128 devices in a mesh: dp: 4 (over z_hi, core), balance: 32 (over y, x, z_lo).
Axes of the slice: x: 4, y: 4, z: 4 (z_hi: 2, z_lo: 2; z = z_hi * 2 + z_lo), core: 2. Of those that a mesh axis runs over, the one named last changes fastest.
Arguments:
- patches: bfloat16 [1024, 256, 1152], P(('dp', 'balance')), may hold values from -6 to 6
- patch_counts: int32 [1024], P(('dp', 'balance')), may hold values from 64 to 256, as said below
- destinations: int32 [1024, 1], P(('dp', 'balance')), may hold values from 0 to 31; in each aligned block of 8 rows (0 to 7, 8 to 15, ...) at most 2 rows name the same one
- image_match: int32 [1024], P(('dp', 'balance')), may hold values from 0 to 1023, each once
- text_features: bfloat16 [1024, 1152], P(('dp', 'balance')), may hold values from -6 to 6
- ln_gain: float32 [1152], replicated, may hold values from 0.25 to 1.75
- w_qkv: bfloat16 [1152, 3456], replicated, may hold values from -0.1875 to 0.1875
- w_out: bfloat16 [1152, 1152], replicated, may hold values from -0.1875 to 0.1875
- logit_scale: float32 [], replicated, may hold values from 2 to 10
- logit_bias: float32 [], replicated, may hold values from -6 to -2
Outputs:
- image_grad: float32 [8192, 1152], P(('dp', 'balance'))
- text_grad: float32 [1024, 1152], P(('dp', 'balance'))
The draws below stay inside these ranges and needn't reach their ends.
Inputs may be any that keep to these rules, and one draw needn't show every extreme that they name: `patch_counts`: each image's first patch is always valid; on every device some image has 256 patches and some 256 // 4. `destinations`: among the images of one device, at most 2 name the same destination, a bound that some block reaches. `image_match`: each text index appears exactly once.
All inputs are finite; a program needn't handle non-finite values.
Results may differ from the reference program's by a relative error of at most 0.0051.
Values may be sent and summed in bfloat16 or wider, within the bound.
A program may use at most 256 MiB of HBM per device.

```python
import math
from functools import partial
import jax
import jax.numpy as jnp
import numpy as np
from jax import lax

D = 1152
HEADS = 16
HEAD = 72
SEQ_LEN = 256
SEQ_DEV = 8
CAP = 2
BUF = 64
IMAGES = 1024
TEXTS = 1024
SLOTS = 8192
N_DP = 4
N_BALANCE = 32


def draw_patch_counts(key, part):
    key = jax.random.fold_in(key, 11)
    heavy_key, count_key = jax.random.split(key)
    quarter = SEQ_LEN // 4
    device_total = IMAGES // SEQ_DEV
    heavy = jax.random.randint(heavy_key, (device_total,), 0, 2)
    heavy_image = jnp.repeat(heavy, SEQ_DEV)
    drawn = quarter + jax.random.randint(count_key, (IMAGES,), 0, quarter + 1) + heavy_image * 2 * quarter
    within = jnp.arange(IMAGES) % SEQ_DEV
    drawn = jnp.where(within == 0, SEQ_LEN, drawn)
    drawn = jnp.where(within == 1, quarter, drawn)
    return drawn.astype(jnp.int32)


def level_of(stream_key, shape, shards, smallest, largest):
    def one(dim, parts):
        steps = jax.random.uniform(jax.random.fold_in(jax.random.fold_in(stream_key, 6), dim), (parts,), jnp.float32, smallest / len(shards), largest / len(shards))
        return jnp.repeat(jnp.exp(steps), shape[dim] // parts).reshape((-1,) + (1,) * (len(shape) - dim - 1))

    level = one(*shards[0])
    for cut in shards[1:]:
        level = level * one(*cut)
    return level


def assign_block(key, own, number, rows, count, top, most, slope):
    order = jax.random.permutation(key, count)
    packed, common = shares(count, rows * top, most, slope, True), shares(count, rows * top, most, slope, False)
    places = jnp.arange(count)

    def named(tallies, offset_by):
        used = int((tallies > 0).sum())
        fixed = max(1, used // 4)
        shifted = fixed + (places - fixed + offset_by * (used - fixed)) % max(1, count - fixed)
        return jnp.zeros((count,), jnp.int32).at[order[jnp.where(places < fixed, places, shifted)]].set(jnp.asarray(tallies, jnp.int32))

    tallies = jnp.where(number % 4 == 0, named(packed, number // 4), named(common, number - number // 4 - 1))
    mixed = jax.random.permutation(jax.random.fold_in(own, 3), count)
    giver, taker = mixed[0:count // 2 * 2:2], mixed[1:count // 2 * 2:2]
    room = jnp.minimum(tallies[giver] - 1, most - tallies[taker]) // 2
    room = jnp.where((giver == order[0]) | (taker == order[0]) | (tallies[taker] == 0), 0, jnp.maximum(room, 0))
    shifted = jax.random.randint(jax.random.fold_in(own, 4), (count // 2,), 0, 1 << 20) % (room + 1)
    tallies = tallies.at[giver].add(-shifted).at[taker].add(shifted)
    labels = jnp.searchsorted(jnp.cumsum(tallies), jnp.arange(rows * top), side="right").astype(jnp.int32)
    table = labels.reshape(top, rows).T
    table = table[jax.random.permutation(jax.random.fold_in(own, 1), rows)]
    offset_by = jax.random.randint(jax.random.fold_in(own, 2), (rows, 1), 0, top)
    return jnp.take_along_axis(table, (jnp.arange(top)[None, :] + offset_by) % top, axis=1)


def shares(count, total, bound, lean, full):
    weights = [(1 << 20) // math.isqrt(grade ** lean) + 1 for grade in range(1, count + 1)]
    largest = bound if full else min(bound, max(-(-total // count), total * weights[0] // sum(weights)))
    least = 1 if total - largest >= count - 1 else 0
    counts, surplus = [largest] + [least] * (count - 1), total - largest - least * (count - 1)
    while surplus > 0:
        candidates = [i for i in range(1, count) if counts[i] < largest] or [i for i in range(1, count) if counts[i] < bound]
        mass, budget = sum([weights[i] for i in candidates]), surplus
        for i in candidates:
            extra = min(bound - counts[i], max(1, budget * weights[i] // mass), surplus)
            counts[i] = counts[i] + extra
            surplus = surplus - extra
    return np.array(counts)


def noise(stream_key, shape, scale, bound, pieces=(), held_as=jnp.bfloat16):
    values = scale * jax.random.normal(stream_key, shape, jnp.float32)
    if pieces:
        values = values * level_of(stream_key, shape, pieces, -0.22, 0.18)
    return jnp.clip(values, -bound, bound).astype(held_as)


def setup_inputs(seed: int = 0) -> dict:
    key_of = jax.random.split(jax.random.key(seed), 11)
    patches = noise(key_of[0], (IMAGES, SEQ_LEN, D), 1.0, 6.0, ((0, 128),))
    patch_counts = draw_patch_counts(jax.random.fold_in(key_of[10], 71), 0)
    destinations_keys = jax.random.split(jax.random.fold_in(key_of[2], 1), IMAGES // SEQ_DEV)
    destinations_turns = jax.random.permutation(jax.random.fold_in(key_of[2], 3), IMAGES // SEQ_DEV)
    destinations = jax.vmap(lambda own, number: assign_block(jax.random.fold_in(key_of[2], 2), own, number, SEQ_DEV, N_BALANCE, 1, CAP, 1))(destinations_keys, destinations_turns).reshape((IMAGES, 1))
    image_match = jax.random.permutation(key_of[3], TEXTS).astype(jnp.int32)
    text_features = noise(key_of[4], (TEXTS, D), 1.0, 6.0, ((0, 128),))
    ln_gain = jnp.clip(1.0 + 0.15 * jax.random.normal(key_of[5], (D,), jnp.float32), 0.25, 1.75)
    w_qkv = noise(key_of[6], (D, 3 * D), D ** -0.5, 0.1875)
    w_out = noise(key_of[7], (D, D), D ** -0.5, 0.1875)
    logit_scale = jnp.clip(jnp.exp(jax.random.uniform(key_of[8], (), jnp.float32, math.log(2.0), math.log(10.0))), 2.0, 10.0)
    logit_bias = jnp.clip(jax.random.uniform(key_of[9], (), jnp.float32, -6.0, -2.0), -6.0, -2.0)
    return {"patches": patches, "patch_counts": patch_counts, "destinations": destinations, "image_match": image_match, "text_features": text_features, "ln_gain": ln_gain, "w_qkv": w_qkv, "w_out": w_out, "logit_scale": logit_scale, "logit_bias": logit_bias}


def layer_norm(rows, gain):
    average = lax.optimization_barrier(jnp.mean(rows, axis=-1, keepdims=True))
    centered = rows - average
    variance = lax.optimization_barrier(jnp.mean(centered * centered, axis=-1, keepdims=True))
    return centered * lax.rsqrt(variance + 1e-06) * gain

def encode_prefix(rows, count, ln_gain, w_qkv, w_out):
    length, model_width = rows.shape
    valid = jnp.maximum(count, 1)
    normed = layer_norm(rows.astype(jnp.float32), ln_gain.astype(jnp.float32)).astype(jnp.bfloat16)
    projected = jnp.dot(normed, w_qkv, preferred_element_type=jnp.float32).astype(jnp.bfloat16)
    projected = projected.reshape(length, 3, HEADS, HEAD)
    queries = projected[:, 0].astype(jnp.float32)
    key_rows = projected[:, 1].astype(jnp.float32)
    value_rows = projected[:, 2].astype(jnp.float32)
    scores = jnp.einsum('qhd,khd->hqk', queries, key_rows) * HEAD ** (-0.5)
    position = jnp.arange(length).astype(jnp.int32)
    live_keys = position < valid
    scores = jnp.where(live_keys[None, None, :], scores, -1e+30)
    row_max = lax.optimization_barrier(jnp.max(scores, axis=-1, keepdims=True))
    expo = jnp.exp(scores - row_max)
    weights = (expo / lax.optimization_barrier(jnp.sum(expo, axis=-1, keepdims=True))).astype(jnp.bfloat16)
    attended = jnp.einsum('hqk,khd->qhd', weights.astype(jnp.float32), value_rows).astype(jnp.bfloat16)
    attended = attended.reshape(length, model_width)
    encoded = rows.astype(jnp.float32) + jnp.dot(attended, w_out, preferred_element_type=jnp.float32)
    summed = lax.optimization_barrier(jnp.sum(jnp.where(live_keys[:, None], encoded, 0.0), axis=0))
    return summed / valid.astype(jnp.float32)

def prefix_branch(size, ln_gain, w_qkv, w_out, operand):
    return encode_prefix(operand[0][:size], operand[1], ln_gain, w_qkv, w_out)

def encode_one(rows, count, ln_gain, w_qkv, w_out):
    quarter = rows.shape[0] // 4
    length_class = ((count + quarter - 1) // quarter).astype(jnp.int32)

    def empty_slot(operand):
        return jnp.zeros((rows.shape[1],), jnp.float32)
    branches = [empty_slot]
    for factor in range(1, 5):
        branches.append(partial(prefix_branch, factor * quarter, ln_gain, w_qkv, w_out))
    return lax.switch(length_class, branches, (rows, count))

def slot_rows(destinations):
    target = destinations[:, 0].reshape(N_DP * N_BALANCE, SEQ_DEV)
    same_dest = target[:, :, None] == target[:, None, :]
    position = jnp.arange(SEQ_DEV).astype(jnp.int32)
    earlier = position[:, None] > position[None, :]
    order_rank = lax.optimization_barrier(jnp.sum(jnp.logical_and(same_dest, earlier[None]), axis=-1)).astype(jnp.int32)
    device = jnp.arange(N_DP * N_BALANCE).astype(jnp.int32)[:, None]
    group = device // N_BALANCE
    source = device % N_BALANCE
    rows = (group * N_BALANCE + target) * BUF + source * CAP + order_rank
    return rows.reshape(-1).astype(jnp.int32)

def reference(patches, patch_counts, destinations, image_match, text_features, ln_gain, w_qkv, w_out, logit_scale, logit_bias):
    model_width = patches.shape[2]
    pooled = lax.map(lambda pair: encode_one(pair[0], pair[1], ln_gain, w_qkv, w_out), (patches, patch_counts))
    image_scale = lax.rsqrt(lax.optimization_barrier(jnp.sum(pooled * pooled, axis=1, keepdims=True)) + 1e-06)
    image_unit = pooled * image_scale
    image_round = image_unit.astype(jnp.bfloat16)
    text_float = text_features.astype(jnp.float32)
    text_scale = lax.rsqrt(lax.optimization_barrier(jnp.sum(text_float * text_float, axis=1, keepdims=True)) + 1e-06)
    text_unit = text_float * text_scale
    text_round = text_unit.astype(jnp.bfloat16)
    logits = logit_scale * jnp.dot(image_round, text_round.T, preferred_element_type=jnp.float32) + logit_bias
    text_index = jnp.arange(TEXTS).astype(jnp.int32)
    pair_sign = jnp.where(image_match[:, None] == text_index[None, :], 1.0, -1.0).astype(jnp.float32)
    pair_weight = (-pair_sign * jax.nn.sigmoid(-pair_sign * logits)).astype(jnp.bfloat16)
    image_dir = logit_scale * jnp.dot(pair_weight, text_round, preferred_element_type=jnp.float32)
    text_dir = logit_scale * jnp.dot(pair_weight.T, image_round, preferred_element_type=jnp.float32)
    image_rows = (image_dir - image_unit * lax.optimization_barrier(jnp.sum(image_unit * image_dir, axis=1, keepdims=True))) * image_scale
    text_grad = (text_dir - text_unit * lax.optimization_barrier(jnp.sum(text_unit * text_dir, axis=1, keepdims=True))) * text_scale
    image_grad = jnp.zeros((SLOTS, model_width), jnp.float32).at[slot_rows(destinations)].set(image_rows)
    return (image_grad, text_grad)
```

```python
import functools
import math

import jax
import jax.numpy as jnp
from jax import lax
from jax.experimental import pallas as pl
from jax.experimental.pallas import tpu as pltpu
from jax.sharding import PartitionSpec as P

HEADS = 16
HEAD = 72
D = 1152
L = 256
SEQ = 8
CAP = 2
N_BAL = 32
ROWS = 16
HALF = 640
REST = D - HALF
F32 = jnp.float32
BF = jnp.bfloat16
NT = (((1,), (1,)), ((), ()))
MESH = pl.DeviceIdType.MESH
QSCALE = HEAD ** -0.5 * math.log2(math.e)
PARTS = ((0, 256, (2, 1, 0)), (256, 256, (1, 0, 2)), (512, 128, (0, 2, 1)))


def pack(rows, extra):
    high = jnp.concatenate([rows[:, HALF:], extra], axis=1)
    return jnp.concatenate([rows[:, :HALF], high], axis=0)


def unpack(block):
    return jnp.concatenate([block[:SEQ], block[SEQ:, :REST]], axis=1)


class Place:
    def __init__(self):
        dp, bal = lax.axis_index("dp"), lax.axis_index("balance")
        self.dp, self.bal = dp, bal
        self.core = lax.rem(dp, 2)
        self.at = (
            lax.div(dp, 2) * 2 + lax.rem(bal, 2),
            lax.div(bal, 8),
            lax.rem(lax.div(bal, 2), 4),
        )

    def device(self, core, z, y, x):
        return (lax.div(z, 2) * 2 + core, (y * 4 + x) * 2 + lax.rem(z, 2))

    def along(self, dim, step):
        at = list(self.at)
        at[dim] = lax.rem(at[dim] + step, 4)
        return self.device(self.core, *at)

    def sibling(self):
        return self.device(1 - self.core, *self.at)


class Gather:
    def __init__(self, place, buf, send, recv):
        self.place, self.buf, self.send, self.recv = place, buf, send, recv

    def hop(self, part, phase):
        lo, width, order = PARTS[part]
        cut = [pl.ds(self.place.at[d], 1) for d in range(3)]
        for d in order[:phase]:
            cut[d] = slice(None)
        if phase == 3:
            cut = [slice(None)] * 3
        block = self.buf.at[self.place.core, cut[0], cut[1], cut[2], :, pl.ds(lo, width)]
        copies = []
        for step in range(1, 4 if phase < 3 else 2):
            index = (part * 4 + phase) * 3 + step - 1
            target = self.place.along(order[phase], step) if phase < 3 else self.place.sibling()
            copies.append(
                pltpu.make_async_remote_copy(
                    src_ref=block,
                    dst_ref=block,
                    send_sem=self.send.at[index],
                    recv_sem=self.recv.at[index],
                    device_id=target,
                    device_id_type=MESH,
                )
            )
        return copies

    def start(self, phase):
        for part in range(3):
            for copy in self.hop(part, phase):
                copy.start()

    def arrive(self, phase):
        for part in range(3):
            for copy in self.hop(part, phase):
                copy.wait_recv()

    def sent(self):
        for phase in range(4):
            for part in range(3):
                for copy in self.hop(part, phase):
                    copy.wait_send()


def ln_block(b, rb, s, cnt, x_v, gain, nm):
    xs = x_v[s, b * rb : (b + 1) * rb, :].astype(F32)
    mu = jnp.sum(xs, axis=1, keepdims=True) * (1.0 / D)
    cen = xs - mu
    var = jnp.sum(cen * cen, axis=1, keepdims=True) * (1.0 / D)
    nm[b * rb : (b + 1) * rb, :] = (cen * lax.rsqrt(var + 1e-6) * gain).astype(BF)
    row = lax.broadcasted_iota(jnp.int32, (rb, 1), 0) + b * rb
    live = jnp.where(row < cnt, xs, 0.0)
    return jnp.sum(live.reshape(rb // 8, 8, D), axis=0)


def ln_stage(s, cnt, x_v, gain_ref, nm, px):
    gain = gain_ref[...].reshape(1, D)
    acc = jnp.zeros((8, D), F32)
    for b in range(8):
        acc = acc + ln_block(b, L // 8, s, cnt, x_v, gain, nm)
    px[pl.ds(s, 1), :] = jnp.sum(acc, axis=0, keepdims=True)


def proj_chunk(n, cnt, nm, w_v, qk):
    lo = n * 256
    p = jnp.dot(nm[...], w_v[:, lo : lo + 256], preferred_element_type=F32)
    lane = lax.broadcasted_iota(jnp.int32, (1, 256), 1) + lo
    if lo < D:
        p = p * jnp.where(lane < D, QSCALE, 1.0)
    if lo + 256 > D:
        keep = lax.broadcasted_iota(jnp.int32, (L, 1), 0) < cnt
        if lo < D:
            keep = jnp.logical_or(keep, lane < D)
        p = jnp.where(keep, p, p[0:1, :])
    qk[:, lo : lo + 256] = p.astype(BF)


def head_stage(h, cnt, qk):
    a = (HEAD * h) // 128 * 128
    b = -(-(HEAD * h + HEAD) // 128) * 128
    lane = lax.broadcasted_iota(jnp.int32, (1, b - a), 1) + a
    mine = jnp.logical_and(lane >= HEAD * h, lane < HEAD * h + HEAD)
    q = qk[:, a:b]
    q = jnp.where(mine, q, jnp.zeros_like(q))
    st = lax.dot_general(qk[:, D + a : D + b], q, NT, preferred_element_type=F32)
    e = jnp.exp2(st - jnp.max(st, axis=0, keepdims=True))
    total = jnp.sum(e, axis=0, keepdims=True) - (L - cnt).astype(F32) * e[0:1, :]
    query = lax.broadcasted_iota(jnp.int32, (1, L), 1)
    p = e * (jnp.where(query < cnt, 1.0, 0.0) / total)
    return jnp.sum(p, axis=1, keepdims=True)


def attend(s, cnt, qk, nm, u):
    head = lax.broadcasted_iota(jnp.int32, (1, 128), 1)
    wbar = jnp.zeros((L, 128), F32)
    for h in range(HEADS):
        wbar = wbar + jnp.where(head == h, head_stage(h, cnt, qk), 0.0)
    key = lax.broadcasted_iota(jnp.int32, (1, L), 1)
    wb = jnp.where(key < cnt, wbar.T[:HEADS], 0.0).astype(BF)
    u[pl.ds(pl.multiple_of(s * HEADS, HEADS), HEADS), :] = jnp.dot(
        wb, nm[...], preferred_element_type=F32
    )


def pool(cs, u, px, w_v, wo_v):
    row = lax.broadcasted_iota(jnp.int32, (SEQ, 1), 0)
    count = jnp.ones((SEQ, 1), F32)
    for i in range(SEQ):
        count = jnp.where(row == i, cs[i].astype(F32), count)
    inv = 1.0 / count
    uu = u[...]
    hi = uu.astype(BF)
    head = lax.broadcasted_iota(jnp.int32, (SEQ, HEADS, 1), 1)
    parts = []
    for n in range(9):
        v = jnp.dot(
            hi, w_v[:, 2 * D + n * 128 : 2 * D + (n + 1) * 128], preferred_element_type=F32
        )
        lane = lax.broadcasted_iota(jnp.int32, (1, 1, 128), 2) + n * 128
        mine = jnp.logical_and(lane >= head * HEAD, lane < head * HEAD + HEAD)
        parts.append(jnp.sum(jnp.where(mine, v.reshape(SEQ, HEADS, 128), 0.0), axis=1))
    att = jnp.concatenate(parts, axis=1) * inv
    ah = att.astype(BF)
    al = (att - ah.astype(F32)).astype(BF)
    o = jnp.dot(jnp.concatenate([ah, al], axis=0), wo_v[...], preferred_element_type=F32)
    return px[...] * inv + o[:SEQ] + o[SEQ:]


def products(mine, plane):
    return [
        lax.dot_general(
            mine, plane(z).reshape(16 * ROWS, HALF), NT, preferred_element_type=F32
        )
        for z in range(4)
    ]


def low_lanes(x):
    return jnp.concatenate([x[:, 8:], x[:, :8]], axis=1)


def high_lanes(x):
    return jnp.concatenate([x[:, -8:], x[:, :-8]], axis=1)


def weigh(prod, scale, bias, paired):
    both = prod[:SEQ] + low_lanes(prod[SEQ:])
    logits = scale * both + bias
    sign = jnp.where(paired, 1.0, -1.0)
    weight = -sign / (1.0 + jnp.exp(sign * logits))
    lane = lax.broadcasted_iota(jnp.int32, weight.shape, 1)
    weight = jnp.where(lax.rem(lane, ROWS) < SEQ, weight, 0.0)
    return jnp.concatenate([weight, high_lanes(weight)], axis=0).astype(BF)


def text_index(core, z):
    lane = lax.broadcasted_iota(jnp.int32, (1, 16 * ROWS), 1)
    dp = (z // 2) * 2 + core
    bal = lax.div(lane, ROWS) * 2 + z % 2
    return (dp * N_BAL + bal) * SEQ + lax.rem(lane, ROWS)


def kernel(
    cs, ms, ds, sc, bi, gain_ref, text_ref, x_h, w_h, wo_h,
    ig_ref, tg_ref,
    x_v, w_v, wo_v, nA, nB, qA, u, px, tbuf, ibuf, mine_t, mine_i, ao, ar,
    sem, tsend, trecv, isend, irecv, asend, arecv,
):
    place = Place()
    core, bal = place.core, place.bal
    scale, bias = sc[0], bi[0]
    copy = pltpu.make_async_copy
    cpx = [copy(x_h.at[i], x_v.at[i], sem.at[i]) for i in range(SEQ)]
    cpw = copy(w_h.at[:, pl.ds(0, 2 * D)], w_v.at[:, pl.ds(0, 2 * D)], sem.at[SEQ])
    cpv = copy(w_h.at[:, pl.ds(2 * D, D)], w_v.at[:, pl.ds(2 * D, D)], sem.at[SEQ + 1])
    cpo = copy(wo_h, wo_v, sem.at[SEQ + 2])
    for c in (cpx[0], cpw, cpx[1], *cpx[2:], cpv, cpo):
        c.start()

    barrier = pltpu.get_barrier_semaphore()

    def greet(device):
        pl.semaphore_signal(barrier, inc=1, device_id=device, device_id_type=MESH)

    def greet_peer(step, carry):
        greet((place.dp, lax.rem(bal + step, N_BAL)))
        return carry

    lax.fori_loop(1, N_BAL, greet_peer, 0)
    z, y, x = place.at
    other = lax.rem(lax.div(z, 2) + 1, 2) * 2
    greet(place.device(core, other, y, x))
    greet(place.device(core, other + 1, y, x))
    greet(place.sibling())

    text = text_ref[...].astype(F32)
    text_scale = lax.rsqrt(jnp.sum(text * text, axis=1, keepdims=True) + 1e-6)
    text_unit = text * text_scale
    row = lax.broadcasted_iota(jnp.int32, (SEQ, 1), 0)
    match = jnp.zeros((SEQ, 1), jnp.int32)
    for i in range(SEQ):
        match = jnp.where(row == i, ms[i], match)
    lane = lax.broadcasted_iota(jnp.int32, (1, 128), 1)
    upper = lax.div(match, 32)
    digits = jnp.where(lane == 0, upper, jnp.where(lane == 1, match - upper * 32, 0))
    block = pack(text_unit, digits.astype(F32)).astype(BF)
    mine_t[...] = block
    tbuf[core, z, y, x] = block

    texts = Gather(place, tbuf, tsend, trecv)
    images = Gather(place, ibuf, isend, irecv)

    cpx[0].wait()
    ln_stage(0, cs[0], x_v, gain_ref, nA, px)
    pl.semaphore_wait(barrier, N_BAL + 2)
    texts.start(0)
    cpw.wait()
    for n in range(9):
        proj_chunk(n, cs[0], nA, w_v, qA)
    cpx[1].wait()
    ln_stage(1, cs[1], x_v, gain_ref, nB, px)
    for c in cpx[2:]:
        c.wait()

    def step(s, now, later):
        n1, n2 = jnp.minimum(s + 1, SEQ - 1), jnp.minimum(s + 2, SEQ - 1)
        attend(s, cs[s], qA, now, u)
        for n in range(9):
            proj_chunk(n, cs[n1], later, w_v, qA)
        ln_stage(n2, cs[n2], x_v, gain_ref, now, px)

    def pair(t, carry):
        step(2 * t, nA, nB)
        step(2 * t + 1, nB, nA)
        for phase in range(3):

            @pl.when(t == phase)
            def _():
                texts.arrive(phase)
                texts.start(phase + 1)

        return carry

    lax.fori_loop(0, SEQ // 2, pair, 0)
    cpv.wait()
    cpo.wait()
    pooled = pool(cs, u, px, w_v, wo_v)

    image_scale = lax.rsqrt(jnp.sum(pooled * pooled, axis=1, keepdims=True) + 1e-6)
    image_unit = pooled * image_scale
    block = pack(image_unit, jnp.zeros((SEQ, 128), F32)).astype(BF)
    mine_i[...] = block
    ibuf[core, z, y, x] = block
    images.start(0)

    texts.arrive(3)

    def image_plane(c):
        prods = products(mine_i[...], lambda zz: tbuf[c, zz])
        total = jnp.zeros((ROWS, HALF), F32)
        for zz in range(4):
            w = weigh(prods[zz], scale, bias, match == text_index(c, zz))
            total = total + jnp.dot(
                w, tbuf[c, zz].reshape(16 * ROWS, HALF), preferred_element_type=F32
            )
        return total

    image_sum = image_plane(0)
    images.arrive(0)
    images.start(1)
    image_sum = image_sum + image_plane(1)
    images.arrive(1)
    images.start(2)
    image_dir = scale * unpack(image_sum)
    grad = (
        image_dir - image_unit * jnp.sum(image_unit * image_dir, axis=1, keepdims=True)
    ) * image_scale
    slot = lax.broadcasted_iota(jnp.int32, (N_BAL * CAP, 1), 0)
    out = jnp.zeros((N_BAL * CAP, D), F32)
    for i in range(SEQ):
        place_i = ds[i, 0] * CAP
        for k in range(i):
            place_i = place_i + jnp.where(ds[k, 0] == ds[i, 0], 1, 0)
        out = out + jnp.where(slot == place_i, grad[i : i + 1], 0.0)
    for c in range(N_BAL):
        ao[c] = out[c * CAP : (c + 1) * CAP]

    def slots(step):
        peer = lax.rem(bal + step, N_BAL)
        return pltpu.make_async_remote_copy(
            src_ref=ao.at[peer],
            dst_ref=ar.at[bal],
            send_sem=asend.at[step],
            recv_sem=arecv.at[step],
            device_id=(place.dp, peer),
            device_id_type=MESH,
        )

    def send_slots(step, carry):
        slots(step).start()
        return carry

    lax.fori_loop(1, N_BAL, send_slots, 0)
    ar[bal] = ao[bal]

    pick = lax.broadcasted_iota(jnp.int32, (ROWS, 128), 1)
    pick = jnp.where(pick == 0, 32.0, jnp.where(pick == 1, 1.0, 0.0)).astype(BF)
    own = (place.dp * N_BAL + bal) * SEQ + row

    def text_plane(c):
        prods = products(mine_t[...], lambda zz: ibuf[c, zz])
        total = jnp.zeros((ROWS, HALF), F32)
        for zz in range(4):
            pairs = lax.dot_general(
                pick,
                tbuf[c, zz, :, :, :, HALF - 128 :].reshape(16 * ROWS, 128),
                NT,
                preferred_element_type=F32,
            )[:SEQ]
            paired = low_lanes(pairs) == own.astype(F32)
            w = weigh(prods[zz], scale, bias, paired)
            total = total + jnp.dot(
                w, ibuf[c, zz].reshape(16 * ROWS, HALF), preferred_element_type=F32
            )
        return total

    images.arrive(2)
    images.start(3)
    text_sum = text_plane(core)
    images.arrive(3)
    text_sum = text_sum + text_plane(1 - core)
    text_dir = scale * unpack(text_sum)
    tg_ref[...] = (
        text_dir - text_unit * jnp.sum(text_unit * text_dir, axis=1, keepdims=True)
    ) * text_scale

    def take_slots(step, carry):
        slots(step).wait()
        return carry

    lax.fori_loop(1, N_BAL, take_slots, 0)
    for c in range(N_BAL):
        ig_ref[c * CAP : (c + 1) * CAP, :] = ar[c]
    texts.sent()
    images.sent()


def body(
    patches, patch_counts, destinations, image_match, text_features,
    ln_gain, w_qkv, w_out, logit_scale, logit_bias,
):
    smem = pl.BlockSpec(memory_space=pltpu.SMEM)
    vmem = pl.BlockSpec(memory_space=pltpu.VMEM)
    hbm = pl.BlockSpec(memory_space=pl.ANY)
    dma = pltpu.SemaphoreType.DMA
    return pl.pallas_call(
        kernel,
        out_shape=(
            jax.ShapeDtypeStruct((N_BAL * CAP, D), F32),
            jax.ShapeDtypeStruct((SEQ, D), F32),
        ),
        in_specs=[smem] * 5 + [vmem] * 2 + [hbm] * 3,
        out_specs=(vmem, vmem),
        scratch_shapes=[
            pltpu.VMEM((SEQ, L, D), BF),
            pltpu.VMEM((D, 3 * D), BF),
            pltpu.VMEM((D, D), BF),
            pltpu.VMEM((L, D), BF),
            pltpu.VMEM((L, D), BF),
            pltpu.VMEM((L, 2 * D), BF),
            pltpu.VMEM((SEQ * HEADS, D), F32),
            pltpu.VMEM((SEQ, D), F32),
            pltpu.VMEM((2, 4, 4, 4, ROWS, HALF), BF),
            pltpu.VMEM((2, 4, 4, 4, ROWS, HALF), BF),
            pltpu.VMEM((ROWS, HALF), BF),
            pltpu.VMEM((ROWS, HALF), BF),
            pltpu.VMEM((N_BAL, CAP, D), F32),
            pltpu.VMEM((N_BAL, CAP, D), F32),
            dma((SEQ + 3,)),
            dma((36,)),
            dma((36,)),
            dma((36,)),
            dma((36,)),
            dma((N_BAL,)),
            dma((N_BAL,)),
        ],
        compiler_params=pltpu.CompilerParams(
            collective_id=0, has_side_effects=True, vmem_limit_bytes=63 * 2**20
        ),
    )(
        patch_counts, image_match, destinations, logit_scale.reshape(1), logit_bias.reshape(1),
        ln_gain, text_features, patches, w_qkv, w_out,
    )


def solution(mesh):
    rows = P(("dp", "balance"))
    return jax.shard_map(
        body,
        mesh=mesh,
        in_specs=(rows,) * 5 + (P(),) * 5,
        out_specs=(rows, rows),
        check_vma=False,
    )
```

```python
import functools
import math

import jax
import jax.numpy as jnp
from jax import lax
from jax.experimental import pallas as pl
from jax.experimental.pallas import tpu as pltpu
from jax.sharding import PartitionSpec as P

HEADS = 16
HEAD = 72
D = 1152
L = 256
SEQ = 8
CAP = 2
N_BAL = 32
ROWS = 16
HALF = 640
REST = D - HALF
F32 = jnp.float32
BF = jnp.bfloat16
NT = (((1,), (1,)), ((), ()))
MESH = pl.DeviceIdType.MESH
QSCALE = HEAD ** -0.5 * math.log2(math.e)
PARTS = ((0, 256, (2, 1, 0)), (256, 256, (1, 0, 2)), (512, 128, (0, 2, 1)))


def pack(rows, extra):
    high = jnp.concatenate([rows[:, HALF:], extra], axis=1)
    return jnp.concatenate([rows[:, :HALF], high], axis=0)


def unpack(block):
    return jnp.concatenate([block[:SEQ], block[SEQ:, :REST]], axis=1)


class Place:
    def __init__(self):
        dp, bal = lax.axis_index("dp"), lax.axis_index("balance")
        self.dp, self.bal = dp, bal
        self.core = lax.rem(dp, 2)
        self.at = (
            lax.div(dp, 2) * 2 + lax.rem(bal, 2),
            lax.div(bal, 8),
            lax.rem(lax.div(bal, 2), 4),
        )

        z, y, x = ([lax.rem(at + k, 4) for k in range(4)] for at in self.at)
        self.dps = [lax.div(at, 2) * 2 + self.core for at in z]
        self.shares = [[lax.rem(at, 2) for at in z], [at * 8 for at in y], [at * 2 for at in x]]

    def chip(self, dz, dy, dx):
        return (self.dps[dz], self.shares[0][dz] + self.shares[1][dy] + self.shares[2][dx])

    def along(self, dim, step):
        steps = [0, 0, 0]
        steps[dim] = step
        return self.chip(*steps)

    def sibling(self):
        return (self.dp + 1 - 2 * self.core, self.bal)


class Gather:
    def __init__(self, place, buf, send, recv):
        self.place, self.buf, self.send, self.recv = place, buf, send, recv
        self.own = [pl.ds(at, 1) for at in place.at]
        self.back = [[pl.ds(lax.rem(at + 4 - k, 4), 1) for k in range(4)] for at in place.at]

    def copy(self, part, phase, step):
        lo, width, order = PARTS[part]
        cut = list(self.own)
        for d in order[:phase]:
            cut[d] = slice(None)
        if phase == 3:
            cut[order[2]] = self.back[order[2]][step]
            target = self.place.sibling()
        else:
            target = self.place.along(order[phase], step)
        block = self.buf.at[self.place.core, cut[0], cut[1], cut[2], :, pl.ds(lo, width)]
        index = (part * 4 + phase) * 4 + step
        return pltpu.make_async_remote_copy(
            src_ref=block,
            dst_ref=block,
            send_sem=self.send.at[index],
            recv_sem=self.recv.at[index],
            device_id=target,
            device_id_type=MESH,
        )

    def start(self, phase):
        for step in range(1, 4):
            for part in range(3):
                self.copy(part, phase, step).start()

    def arrive(self, phase):
        for step in range(0 if phase == 3 else 1, 4):
            for part in range(3):
                self.copy(part, phase, step).wait_recv()

    def share_own(self):
        for part in range(3):
            self.copy(part, 3, 0).start()

    def share(self):
        for step in (1, 3, 2):
            for part in range(3):
                self.copy(part, 2, step).wait_recv()
                self.copy(part, 3, step).start()

    def sent(self):
        for phase in range(4):
            for step in range(0 if phase == 3 else 1, 4):
                for part in range(3):
                    self.copy(part, phase, step).wait_send()


def ln_block(b, rb, s, cnt, x_v, gain, nm):
    xs = x_v[s, b * rb : (b + 1) * rb, :].astype(F32)
    mu = jnp.sum(xs, axis=1, keepdims=True) * (1.0 / D)
    cen = xs - mu
    var = jnp.sum(cen * cen, axis=1, keepdims=True) * (1.0 / D)
    nm[b * rb : (b + 1) * rb, :] = (cen * lax.rsqrt(var + 1e-6) * gain).astype(BF)
    row = lax.broadcasted_iota(jnp.int32, (rb, 1), 0) + b * rb
    live = jnp.where(row < cnt, xs, 0.0)
    return jnp.sum(live.reshape(rb // 8, 8, D), axis=0)


def ln_stage(s, cnt, x_v, gain_ref, nm, px):
    gain = gain_ref[...].reshape(1, D)
    acc = jnp.zeros((8, D), F32)
    for b in range(8):
        acc = acc + ln_block(b, L // 8, s, cnt, x_v, gain, nm)
    px[pl.ds(s, 1), :] = jnp.sum(acc, axis=0, keepdims=True)


def proj_chunk(n, cnt, nm, w_v, qk):
    lo = n * 256
    p = jnp.dot(nm[...], w_v[:, lo : lo + 256], preferred_element_type=F32)
    lane = lax.broadcasted_iota(jnp.int32, (1, 256), 1) + lo
    if lo < D:
        p = p * jnp.where(lane < D, QSCALE, 1.0)
    if lo + 256 > D:
        keep = lax.broadcasted_iota(jnp.int32, (L, 1), 0) < cnt
        if lo < D:
            keep = jnp.logical_or(keep, lane < D)
        p = jnp.where(keep, p, p[0:1, :])
    qk[:, lo : lo + 256] = p.astype(BF)


def head_stage(h, cnt, qk):
    a = (HEAD * h) // 128 * 128
    b = -(-(HEAD * h + HEAD) // 128) * 128
    lane = lax.broadcasted_iota(jnp.int32, (1, b - a), 1) + a
    mine = jnp.logical_and(lane >= HEAD * h, lane < HEAD * h + HEAD)
    q = qk[:, a:b]
    q = jnp.where(mine, q, jnp.zeros_like(q))
    st = lax.dot_general(qk[:, D + a : D + b], q, NT, preferred_element_type=F32)
    e = jnp.exp2(st - jnp.max(st, axis=0, keepdims=True))
    total = jnp.sum(e, axis=0, keepdims=True) - (L - cnt).astype(F32) * e[0:1, :]
    query = lax.broadcasted_iota(jnp.int32, (1, L), 1)
    p = e * (jnp.where(query < cnt, 1.0, 0.0) / total)
    return jnp.sum(p, axis=1, keepdims=True)


def attend(s, cnt, qk, nm, u):
    head = lax.broadcasted_iota(jnp.int32, (1, 128), 1)
    wbar = jnp.zeros((L, 128), F32)
    for h in range(HEADS):
        wbar = wbar + jnp.where(head == h, head_stage(h, cnt, qk), 0.0)
    key = lax.broadcasted_iota(jnp.int32, (1, L), 1)
    wb = jnp.where(key < cnt, wbar.T[:HEADS], 0.0).astype(BF)
    u[pl.ds(pl.multiple_of(s * HEADS, HEADS), HEADS), :] = jnp.dot(
        wb, nm[...], preferred_element_type=F32
    )


def pool(cs, u, px, w_v, wo_v):
    row = lax.broadcasted_iota(jnp.int32, (SEQ, 1), 0)
    count = jnp.ones((SEQ, 1), F32)
    for i in range(SEQ):
        count = jnp.where(row == i, cs[i].astype(F32), count)
    inv = 1.0 / count
    uu = u[...]
    hi = uu.astype(BF)
    both = jnp.concatenate([hi, (uu - hi.astype(F32)).astype(BF)], axis=0)
    head = lax.broadcasted_iota(jnp.int32, (SEQ, HEADS, 1), 1)
    parts = []
    for n in range(9):
        v = jnp.dot(
            both, w_v[:, 2 * D + n * 128 : 2 * D + (n + 1) * 128], preferred_element_type=F32
        )
        v = v[: SEQ * HEADS] + v[SEQ * HEADS :]
        lane = lax.broadcasted_iota(jnp.int32, (1, 1, 128), 2) + n * 128
        mine = jnp.logical_and(lane >= head * HEAD, lane < head * HEAD + HEAD)
        parts.append(jnp.sum(jnp.where(mine, v.reshape(SEQ, HEADS, 128), 0.0), axis=1))
    att = jnp.concatenate(parts, axis=1) * inv
    ah = att.astype(BF)
    al = (att - ah.astype(F32)).astype(BF)
    o = jnp.dot(jnp.concatenate([ah, al], axis=0), wo_v[...], preferred_element_type=F32)
    return px[...] * inv + o[:SEQ] + o[SEQ:]


def products(mine, plane):
    return [
        lax.dot_general(
            mine, plane(z).reshape(16 * ROWS, HALF), NT, preferred_element_type=F32
        )
        for z in range(4)
    ]


def low_lanes(x):
    return jnp.concatenate([x[:, 8:], x[:, :8]], axis=1)


def high_lanes(x):
    return jnp.concatenate([x[:, -8:], x[:, :-8]], axis=1)


def weigh(prod, scale, bias, paired):
    both = prod[:SEQ] + low_lanes(prod[SEQ:])
    logits = scale * both + bias
    sign = jnp.where(paired, 1.0, -1.0)
    weight = -sign / (1.0 + jnp.exp(sign * logits))
    lane = lax.broadcasted_iota(jnp.int32, weight.shape, 1)
    weight = jnp.where(lax.rem(lane, ROWS) < SEQ, weight, 0.0)
    return jnp.concatenate([weight, high_lanes(weight)], axis=0).astype(BF)


def text_index(core, z):
    lane = lax.broadcasted_iota(jnp.int32, (1, 16 * ROWS), 1)
    dp = (z // 2) * 2 + core
    bal = lax.div(lane, ROWS) * 2 + z % 2
    return (dp * N_BAL + bal) * SEQ + lax.rem(lane, ROWS)


def kernel(
    cs, ms, ds, sc, bi, gain_ref, text_ref, x_h, w_h, wo_h,
    ig_ref, tg_ref,
    x_v, w_v, wo_v, nA, nB, qA, u, px, tbuf, ibuf, mine_t, mine_i, ao, ar,
    sem, tsend, trecv, isend, irecv, asend, arecv,
):
    place = Place()
    core, bal = place.core, place.bal
    scale, bias = sc[0], bi[0]
    copy = pltpu.make_async_copy
    cpx = [copy(x_h.at[i], x_v.at[i], sem.at[i]) for i in range(SEQ)]
    cpw = copy(w_h.at[:, pl.ds(0, 2 * D)], w_v.at[:, pl.ds(0, 2 * D)], sem.at[SEQ])
    cpv = copy(w_h.at[:, pl.ds(2 * D, D)], w_v.at[:, pl.ds(2 * D, D)], sem.at[SEQ + 1])
    cpo = copy(wo_h, wo_v, sem.at[SEQ + 2])
    for c in (cpx[0], cpw, cpx[1], *cpx[2:], cpv, cpo):
        c.start()

    barrier = pltpu.get_barrier_semaphore()

    def greet(device):
        pl.semaphore_signal(barrier, inc=1, device_id=device, device_id_type=MESH)

    z, y, x = place.at
    peers = [lax.rem(bal + k, N_BAL) for k in range(N_BAL)]
    for k in range(1, N_BAL):
        greet((place.dp, peers[k]))
    far = lax.rem(lax.div(z, 2) + 1, 2) * 2 + core
    greet((far, bal))
    greet((far, bal + 1 - 2 * lax.rem(z, 2)))
    greet(place.sibling())

    text = text_ref[...].astype(F32)
    text_scale = lax.rsqrt(jnp.sum(text * text, axis=1, keepdims=True) + 1e-6)
    text_unit = text * text_scale
    row = lax.broadcasted_iota(jnp.int32, (SEQ, 1), 0)
    match = jnp.zeros((SEQ, 1), jnp.int32)
    for i in range(SEQ):
        match = jnp.where(row == i, ms[i], match)
    lane = lax.broadcasted_iota(jnp.int32, (1, 128), 1)
    upper = lax.div(match, 32)
    digits = jnp.where(lane == 0, upper, jnp.where(lane == 1, match - upper * 32, 0))
    block = pack(text_unit, digits.astype(F32)).astype(BF)
    mine_t[...] = block
    tbuf[core, z, y, x] = block

    texts = Gather(place, tbuf, tsend, trecv)
    images = Gather(place, ibuf, isend, irecv)

    cpx[0].wait()
    ln_stage(0, cs[0], x_v, gain_ref, nA, px)
    pl.semaphore_wait(barrier, N_BAL + 2)
    texts.start(0)
    cpw.wait()
    for n in range(9):
        proj_chunk(n, cs[0], nA, w_v, qA)
    cpx[1].wait()
    ln_stage(1, cs[1], x_v, gain_ref, nB, px)
    for c in cpx[2:]:
        c.wait()

    def step(s, now, later):
        attend(s, cs[s], qA, now, u)
        for n in range(9):
            proj_chunk(n, cs[s + 1], later, w_v, qA)
        ln_stage(s + 2, cs[s + 2], x_v, gain_ref, now, px)

    def pair(t, carry):
        step(2 * t, nA, nB)
        step(2 * t + 1, nB, nA)

        @pl.when(t == 0)
        def _():
            texts.arrive(0)
            texts.start(1)

        @pl.when(t == 1)
        def _():
            texts.arrive(1)
            texts.start(2)
            texts.share_own()

        @pl.when(t == 2)
        def _():
            texts.share()

        return carry

    lax.fori_loop(0, SEQ // 2 - 1, pair, 0)
    attend(SEQ - 2, cs[SEQ - 2], qA, nA, u)
    for n in range(9):
        proj_chunk(n, cs[SEQ - 1], nB, w_v, qA)
    attend(SEQ - 1, cs[SEQ - 1], qA, nB, u)
    cpv.wait()
    cpo.wait()
    pooled = pool(cs, u, px, w_v, wo_v)

    image_scale = lax.rsqrt(jnp.sum(pooled * pooled, axis=1, keepdims=True) + 1e-6)
    image_unit = pooled * image_scale
    block = pack(image_unit, jnp.zeros((SEQ, 128), F32)).astype(BF)
    mine_i[...] = block
    ibuf[core, z, y, x] = block
    images.start(0)

    texts.arrive(3)

    def image_plane(c):
        prods = products(mine_i[...], lambda zz: tbuf[c, zz])
        total = jnp.zeros((ROWS, HALF), F32)
        for zz in range(4):
            w = weigh(prods[zz], scale, bias, match == text_index(c, zz))
            total = total + jnp.dot(
                w, tbuf[c, zz].reshape(16 * ROWS, HALF), preferred_element_type=F32
            )
        return total

    image_sum = image_plane(0)
    images.arrive(0)
    images.start(1)
    image_sum = image_sum + image_plane(1)
    images.arrive(1)
    images.start(2)
    images.share_own()
    image_dir = scale * unpack(image_sum)
    grad = (
        image_dir - image_unit * jnp.sum(image_unit * image_dir, axis=1, keepdims=True)
    ) * image_scale
    slot = lax.broadcasted_iota(jnp.int32, (N_BAL * CAP, 1), 0)
    out = jnp.zeros((N_BAL * CAP, D), F32)
    for i in range(SEQ):
        place_i = ds[i] * CAP
        for k in range(i):
            place_i = place_i + jnp.where(ds[k] == ds[i], 1, 0)
        out = out + jnp.where(slot == place_i, grad[i : i + 1], 0.0)
    for c in range(N_BAL):
        ao[c] = out[c * CAP : (c + 1) * CAP]

    def slots(step):
        return pltpu.make_async_remote_copy(
            src_ref=ao.at[peers[step]],
            dst_ref=ar.at[bal],
            send_sem=asend.at[step],
            recv_sem=arecv.at[step],
            device_id=(place.dp, peers[step]),
            device_id_type=MESH,
        )

    for k in range(1, N_BAL):
        slots(k).start()
    ar[bal] = ao[bal]

    pick = lax.broadcasted_iota(jnp.int32, (ROWS, 128), 1)
    pick = jnp.where(pick == 0, 32.0, jnp.where(pick == 1, 1.0, 0.0)).astype(BF)
    own = (place.dp * N_BAL + bal) * SEQ + row

    def text_plane(c):
        prods = products(mine_t[...], lambda zz: ibuf[c, zz])
        total = jnp.zeros((ROWS, HALF), F32)
        for zz in range(4):
            pairs = lax.dot_general(
                pick,
                tbuf[c, zz, :, :, :, HALF - 128 :].reshape(16 * ROWS, 128),
                NT,
                preferred_element_type=F32,
            )[:SEQ]
            paired = low_lanes(pairs) == own.astype(F32)
            w = weigh(prods[zz], scale, bias, paired)
            total = total + jnp.dot(
                w, ibuf[c, zz].reshape(16 * ROWS, HALF), preferred_element_type=F32
            )
        return total

    images.share()
    text_sum = text_plane(core)
    images.arrive(3)
    text_sum = text_sum + text_plane(1 - core)
    text_dir = scale * unpack(text_sum)
    tg_ref[...] = (
        text_dir - text_unit * jnp.sum(text_unit * text_dir, axis=1, keepdims=True)
    ) * text_scale

    for k in range(1, N_BAL):
        slots(k).wait()
    for c in range(N_BAL):
        ig_ref[c * CAP : (c + 1) * CAP, :] = ar[c]
    texts.sent()
    images.sent()


def deliver(ig, tg, ig_out, tg_out):
    ig_out[...] = ig[...]
    tg_out[...] = tg[...]


def body(
    patches, patch_counts, destinations, image_match, text_features,
    ln_gain, w_qkv, w_out, logit_scale, logit_bias,
):
    smem = pl.BlockSpec(memory_space=pltpu.SMEM)
    vmem = pl.BlockSpec(memory_space=pltpu.VMEM)
    hbm = pl.BlockSpec(memory_space=pl.ANY)
    dma = pltpu.SemaphoreType.DMA
    out_shape = (
        jax.ShapeDtypeStruct((N_BAL * CAP, D), F32),
        jax.ShapeDtypeStruct((SEQ, D), F32),
    )
    grads = pl.pallas_call(
        kernel,
        out_shape=out_shape,
        in_specs=[smem] * 5 + [vmem] * 2 + [hbm] * 3,
        out_specs=(vmem, vmem),
        scratch_shapes=[
            pltpu.VMEM((SEQ, L, D), BF),
            pltpu.VMEM((D, 3 * D), BF),
            pltpu.VMEM((D, D), BF),
            pltpu.VMEM((L, D), BF),
            pltpu.VMEM((L, D), BF),
            pltpu.VMEM((L, 2 * D), BF),
            pltpu.VMEM((SEQ * HEADS, D), F32),
            pltpu.VMEM((SEQ, D), F32),
            pltpu.VMEM((2, 4, 4, 4, ROWS, HALF), BF),
            pltpu.VMEM((2, 4, 4, 4, ROWS, HALF), BF),
            pltpu.VMEM((ROWS, HALF), BF),
            pltpu.VMEM((ROWS, HALF), BF),
            pltpu.VMEM((N_BAL, CAP, D), F32),
            pltpu.VMEM((N_BAL, CAP, D), F32),
            dma((SEQ + 3,)),
            dma((48,)),
            dma((48,)),
            dma((48,)),
            dma((48,)),
            dma((N_BAL,)),
            dma((N_BAL,)),
        ],
        compiler_params=pltpu.CompilerParams(
            collective_id=0, has_side_effects=True, vmem_limit_bytes=63 * 2**20
        ),
    )(
        patch_counts, image_match, destinations.reshape(SEQ), logit_scale.reshape(1), logit_bias.reshape(1),
        ln_gain, text_features, patches, w_qkv, w_out,
    )
    return pl.pallas_call(
        deliver,
        out_shape=out_shape,
        in_specs=[vmem] * 2,
        out_specs=(vmem, vmem),
    )(*grads)


def solution(mesh):
    rows = P(("dp", "balance"))
    return jax.shard_map(
        body,
        mesh=mesh,
        in_specs=(rows,) * 5 + (P(),) * 5,
        out_specs=(rows, rows),
        check_vma=False,
    )
```

```python
import functools
import math

import jax
import jax.numpy as jnp
from jax import lax
from jax.experimental import pallas as pl
from jax.experimental.pallas import tpu as pltpu
from jax.sharding import PartitionSpec as P

HEADS = 16
HEAD = 72
D = 1152
L = 256
SEQ = 8
CAP = 2
N_BAL = 32
ROWS = 16
HALF = 640
REST = D - HALF
F32 = jnp.float32
BF = jnp.bfloat16
NT = (((1,), (1,)), ((), ()))
MESH = pl.DeviceIdType.MESH
QSCALE = HEAD ** -0.5 * math.log2(math.e)
PARTS = ((0, 256, (2, 1, 0)), (256, 256, (1, 0, 2)), (512, 128, (0, 2, 1)))


def pack(rows, extra):
    high = jnp.concatenate([rows[:, HALF:], extra], axis=1)
    return jnp.concatenate([rows[:, :HALF], high], axis=0)


def unpack(block):
    return jnp.concatenate([block[:SEQ], block[SEQ:, :REST]], axis=1)


class Place:
    def __init__(self):
        dp, bal = lax.axis_index("dp"), lax.axis_index("balance")
        self.dp, self.bal = dp, bal
        self.core = lax.rem(dp, 2)
        self.at = (
            lax.div(dp, 2) * 2 + lax.rem(bal, 2),
            lax.div(bal, 8),
            lax.rem(lax.div(bal, 2), 4),
        )

        z, y, x = ([lax.rem(at + k, 4) for k in range(4)] for at in self.at)
        self.dps = [lax.div(at, 2) * 2 + self.core for at in z]
        self.shares = [[lax.rem(at, 2) for at in z], [at * 8 for at in y], [at * 2 for at in x]]

    def chip(self, dz, dy, dx):
        return (self.dps[dz], self.shares[0][dz] + self.shares[1][dy] + self.shares[2][dx])

    def along(self, dim, step):
        steps = [0, 0, 0]
        steps[dim] = step
        return self.chip(*steps)

    def sibling(self):
        return (self.dp + 1 - 2 * self.core, self.bal)


class Gather:
    def __init__(self, place, buf, send, recv):
        self.place, self.buf, self.send, self.recv = place, buf, send, recv
        self.own = [pl.ds(at, 1) for at in place.at]
        self.back = [[pl.ds(lax.rem(at + 4 - k, 4), 1) for k in range(4)] for at in place.at]

    def copy(self, part, phase, step):
        lo, width, order = PARTS[part]
        cut = list(self.own)
        for d in order[:phase]:
            cut[d] = slice(None)
        if phase == 3:
            cut[order[2]] = self.back[order[2]][step]
            target = self.place.sibling()
        else:
            target = self.place.along(order[phase], step)
        block = self.buf.at[self.place.core, cut[0], cut[1], cut[2], :, pl.ds(lo, width)]
        index = (part * 4 + phase) * 4 + step
        return pltpu.make_async_remote_copy(
            src_ref=block,
            dst_ref=block,
            send_sem=self.send.at[index],
            recv_sem=self.recv.at[index],
            device_id=target,
            device_id_type=MESH,
        )

    def start(self, phase):
        for step in range(1, 4):
            for part in range(3):
                self.copy(part, phase, step).start()

    def arrive(self, phase):
        for step in range(0 if phase == 3 else 1, 4):
            for part in range(3):
                self.copy(part, phase, step).wait_recv()

    def share_own(self):
        for part in range(3):
            self.copy(part, 3, 0).start()

    def share(self):
        for step in (1, 3, 2):
            for part in range(3):
                self.copy(part, 2, step).wait_recv()
                self.copy(part, 3, step).start()

    def sent(self, first, last):
        for phase in range(first, last):
            for step in range(0 if phase == 3 else 1, 4):
                for part in range(3):
                    self.copy(part, phase, step).wait_send()


def ln_block(b, rb, s, cnt, x_v, gain, nm):
    xs = x_v[s, b * rb : (b + 1) * rb, :].astype(F32)
    mu = jnp.sum(xs, axis=1, keepdims=True) * (1.0 / D)
    cen = xs - mu
    var = jnp.sum(cen * cen, axis=1, keepdims=True) * (1.0 / D)
    nm[b * rb : (b + 1) * rb, :] = (cen * lax.rsqrt(var + 1e-6) * gain).astype(BF)
    row = lax.broadcasted_iota(jnp.int32, (rb, 1), 0) + b * rb
    live = jnp.where(row < cnt, xs, 0.0)
    return jnp.sum(live.reshape(rb // 8, 8, D), axis=0)


def ln_stage(s, cnt, x_v, gain_ref, nm, px):
    gain = gain_ref[...].reshape(1, D)
    acc = jnp.zeros((8, D), F32)
    for b in range(8):
        acc = acc + ln_block(b, L // 8, s, cnt, x_v, gain, nm)
    px[pl.ds(s, 1), :] = jnp.sum(acc, axis=0, keepdims=True)


def proj_chunk(n, cnt, nm, w_v, qk):
    lo = n * 256
    p = jnp.dot(nm[...], w_v[:, lo : lo + 256], preferred_element_type=F32)
    lane = lax.broadcasted_iota(jnp.int32, (1, 256), 1) + lo
    if lo < D:
        p = p * jnp.where(lane < D, QSCALE, 1.0)
    if lo + 256 > D:
        keep = lax.broadcasted_iota(jnp.int32, (L, 1), 0) < cnt
        if lo < D:
            keep = jnp.logical_or(keep, lane < D)
        p = jnp.where(keep, p, p[0:1, :])
    qk[:, lo : lo + 256] = p.astype(BF)


def head_stage(h, cnt, qk):
    a = (HEAD * h) // 128 * 128
    b = -(-(HEAD * h + HEAD) // 128) * 128
    lane = lax.broadcasted_iota(jnp.int32, (1, b - a), 1) + a
    mine = jnp.logical_and(lane >= HEAD * h, lane < HEAD * h + HEAD)
    q = qk[:, a:b]
    q = jnp.where(mine, q, jnp.zeros_like(q))
    st = lax.dot_general(qk[:, D + a : D + b], q, NT, preferred_element_type=F32)
    e = jnp.exp2(st - jnp.max(st, axis=0, keepdims=True))
    total = jnp.sum(e, axis=0, keepdims=True) - (L - cnt).astype(F32) * e[0:1, :]
    query = lax.broadcasted_iota(jnp.int32, (1, L), 1)
    p = e * (jnp.where(query < cnt, 1.0, 0.0) / total)
    return jnp.sum(p, axis=1, keepdims=True)


def attend(s, cnt, qk, nm, u, wsum):
    for h in range(HEADS):
        wsum[:, h : h + 1] = head_stage(h, cnt, qk)
    key = lax.broadcasted_iota(jnp.int32, (1, L), 1)
    wb = jnp.where(key < cnt, wsum[...].T[:HEADS], 0.0).astype(BF)
    u[pl.ds(pl.multiple_of(s * HEADS, HEADS), HEADS), :] = jnp.dot(
        wb, nm[...], preferred_element_type=F32
    )


def pool(cs, u, px, w_v, wo_v):
    row = lax.broadcasted_iota(jnp.int32, (SEQ, 1), 0)
    count = jnp.ones((SEQ, 1), F32)
    for i in range(SEQ):
        count = jnp.where(row == i, cs[i].astype(F32), count)
    inv = 1.0 / count
    uu = u[...]
    hi = uu.astype(BF)
    both = jnp.concatenate([hi, (uu - hi.astype(F32)).astype(BF)], axis=0)
    head = lax.broadcasted_iota(jnp.int32, (SEQ, HEADS, 1), 1)
    parts = []
    for lo in range(0, D, 256):
        width = min(256, D - lo)
        v = jnp.dot(
            both, w_v[:, 2 * D + lo : 2 * D + lo + width], preferred_element_type=F32
        )
        v = v[: SEQ * HEADS] + v[SEQ * HEADS :]
        lane = lax.broadcasted_iota(jnp.int32, (1, 1, width), 2) + lo
        mine = jnp.logical_and(lane >= head * HEAD, lane < head * HEAD + HEAD)
        parts.append(jnp.sum(jnp.where(mine, v.reshape(SEQ, HEADS, width), 0.0), axis=1))
    att = jnp.concatenate(parts, axis=1) * inv
    ah = att.astype(BF)
    al = (att - ah.astype(F32)).astype(BF)
    o = jnp.dot(jnp.concatenate([ah, al], axis=0), wo_v[...], preferred_element_type=F32)
    return px[...] * inv + o[:SEQ] + o[SEQ:]


def products(mine, plane):
    return [
        lax.dot_general(
            mine, plane(z).reshape(16 * ROWS, HALF), NT, preferred_element_type=F32
        )
        for z in range(4)
    ]


def low_lanes(x):
    return jnp.concatenate([x[:, 8:], x[:, :8]], axis=1)


def high_lanes(x):
    return jnp.concatenate([x[:, -8:], x[:, :-8]], axis=1)


def weigh(prod, scale, bias, paired):
    both = prod[:SEQ] + low_lanes(prod[SEQ:])
    logits = scale * both + bias
    sign = jnp.where(paired, 1.0, -1.0)
    weight = -sign / (1.0 + jnp.exp(sign * logits))
    lane = lax.broadcasted_iota(jnp.int32, weight.shape, 1)
    weight = jnp.where(lax.rem(lane, ROWS) < SEQ, weight, 0.0)
    return jnp.concatenate([weight, high_lanes(weight)], axis=0).astype(BF)


def text_index(core, z):
    lane = lax.broadcasted_iota(jnp.int32, (1, 16 * ROWS), 1)
    dp = (z // 2) * 2 + core
    bal = lax.div(lane, ROWS) * 2 + z % 2
    return (dp * N_BAL + bal) * SEQ + lax.rem(lane, ROWS)


def kernel(
    cs, ms, ds, sc, bi, gain_ref, text_ref, x_h, w_h, wo_h,
    ig_ref, tg_ref,
    x_v, w_v, wo_v, nA, nB, qA, qB, wsA, wsB, u, px, tbuf, ibuf, mine_t, mine_i, pairs_v, ao, ar,
    sem, tsend, trecv, isend, irecv, asend, arecv,
):
    place = Place()
    core, bal = place.core, place.bal
    scale, bias = sc[0], bi[0]
    copy = pltpu.make_async_copy
    cpx = [copy(x_h.at[i], x_v.at[i], sem.at[i]) for i in range(SEQ)]
    cpw = copy(w_h.at[:, pl.ds(0, 2 * D)], w_v.at[:, pl.ds(0, 2 * D)], sem.at[SEQ])
    cpv = copy(w_h.at[:, pl.ds(2 * D, D)], w_v.at[:, pl.ds(2 * D, D)], sem.at[SEQ + 1])
    cpo = copy(wo_h, wo_v, sem.at[SEQ + 2])
    cpx[0].start()
    cpw.start()
    for c in (*cpx[1:], cpv, cpo):
        c.start()

    barrier = pltpu.get_barrier_semaphore()

    def greet(device):
        pl.semaphore_signal(barrier, inc=1, device_id=device, device_id_type=MESH)

    z, y, x = place.at
    peers = [lax.rem(bal + k, N_BAL) for k in range(N_BAL)]
    for k in range(1, N_BAL):
        greet((place.dp, peers[k]))
    far = lax.rem(lax.div(z, 2) + 1, 2) * 2 + core
    greet((far, bal))
    greet((far, bal + 1 - 2 * lax.rem(z, 2)))
    greet(place.sibling())

    text = text_ref[...].astype(F32)
    text_scale = lax.rsqrt(jnp.sum(text * text, axis=1, keepdims=True) + 1e-6)
    text_unit = text * text_scale
    row = lax.broadcasted_iota(jnp.int32, (SEQ, 1), 0)
    match = jnp.zeros((SEQ, 1), jnp.int32)
    for i in range(SEQ):
        match = jnp.where(row == i, ms[i], match)
    lane = lax.broadcasted_iota(jnp.int32, (1, 128), 1)
    upper = lax.div(match, 32)
    digits = jnp.where(lane == 0, upper, jnp.where(lane == 1, match - upper * 32, 0))
    block = pack(text_unit, digits.astype(F32)).astype(BF)
    mine_t[...] = block
    tbuf[core, z, y, x] = block

    texts = Gather(place, tbuf, tsend, trecv)
    images = Gather(place, ibuf, isend, irecv)

    cpx[0].wait()
    ln_stage(0, cs[0], x_v, gain_ref, nA, px)
    pl.semaphore_wait(barrier, N_BAL + 2)
    texts.start(0)
    cpw.wait()
    for n in range(9):
        proj_chunk(n, cs[0], nA, w_v, qA)
    cpx[1].wait()
    ln_stage(1, cs[1], x_v, gain_ref, nB, px)

    def step(s, now, later, qk, qk_later, wsum):
        for n in range(9):
            proj_chunk(n, cs[s + 1], later, w_v, qk_later)
        attend(s, cs[s], qk, now, u, wsum)
        copy(x_h.at[s + 2], x_v.at[s + 2], sem.at[s + 2]).wait()
        ln_stage(s + 2, cs[s + 2], x_v, gain_ref, now, px)

    def pair(t, carry):
        step(2 * t, nA, nB, qA, qB, wsA)
        step(2 * t + 1, nB, nA, qB, qA, wsB)

        @pl.when(t == 0)
        def _():
            texts.arrive(0)
            texts.start(1)

        @pl.when(t == 1)
        def _():
            texts.arrive(1)
            texts.start(2)
            texts.share_own()

        @pl.when(t == 2)
        def _():
            texts.share()

        return carry

    lax.fori_loop(0, SEQ // 2 - 1, pair, 0)
    for n in range(9):
        proj_chunk(n, cs[SEQ - 1], nB, w_v, qB)
    attend(SEQ - 2, cs[SEQ - 2], qA, nA, u, wsA)
    attend(SEQ - 1, cs[SEQ - 1], qB, nB, u, wsB)
    cpv.wait()
    cpo.wait()
    pooled = pool(cs, u, px, w_v, wo_v)

    image_scale = lax.rsqrt(jnp.sum(pooled * pooled, axis=1, keepdims=True) + 1e-6)
    image_unit = pooled * image_scale
    block = pack(image_unit, jnp.zeros((SEQ, 128), F32)).astype(BF)
    mine_i[...] = block
    ibuf[core, z, y, x] = block
    images.start(0)
    texts.sent(0, 4)

    texts.arrive(3)

    def image_plane(c):
        prods = products(mine_i[...], lambda zz: tbuf[c, zz])
        total = jnp.zeros((ROWS, HALF), F32)
        for zz in range(4):
            w = weigh(prods[zz], scale, bias, match == text_index(c, zz))
            total = total + jnp.dot(
                w, tbuf[c, zz].reshape(16 * ROWS, HALF), preferred_element_type=F32
            )
        return total

    image_sum = image_plane(0)
    images.arrive(0)
    images.start(1)
    image_sum = image_sum + image_plane(1)
    images.arrive(1)
    images.start(2)
    images.share_own()
    image_dir = scale * unpack(image_sum)
    grad = (
        image_dir - image_unit * jnp.sum(image_unit * image_dir, axis=1, keepdims=True)
    ) * image_scale
    slot = lax.broadcasted_iota(jnp.int32, (N_BAL * CAP, 1), 0)
    out = jnp.zeros((N_BAL * CAP, D), F32)
    for i in range(SEQ):
        place_i = ds[i] * CAP
        for k in range(i):
            place_i = place_i + jnp.where(ds[k] == ds[i], 1, 0)
        out = out + jnp.where(slot == place_i, grad[i : i + 1], 0.0)
    for c in range(N_BAL):
        ao[c] = out[c * CAP : (c + 1) * CAP]

    def slots(step):
        return pltpu.make_async_remote_copy(
            src_ref=ao.at[peers[step]],
            dst_ref=ar.at[bal],
            send_sem=asend.at[step],
            recv_sem=arecv.at[step],
            device_id=(place.dp, peers[step]),
            device_id_type=MESH,
        )

    for k in range(1, N_BAL):
        slots(k).start()
    ar[bal] = ao[bal]

    pick = lax.broadcasted_iota(jnp.int32, (ROWS, 128), 1)
    pick = jnp.where(pick == 0, 32.0, jnp.where(pick == 1, 1.0, 0.0)).astype(BF)
    own = ((place.dp * N_BAL + bal) * SEQ + row).astype(F32)
    for c in range(2):
        for zz in range(4):
            digits = tbuf[c, zz, :, :, :, HALF - 128 :].reshape(16 * ROWS, 128)
            pairs = lax.dot_general(pick, digits, NT, preferred_element_type=F32)
            pairs_v[c, zz] = low_lanes(pairs[:SEQ])

    def text_plane(c):
        prods = products(mine_t[...], lambda zz: ibuf[c, zz])
        total = jnp.zeros((ROWS, HALF), F32)
        for zz in range(4):
            w = weigh(prods[zz], scale, bias, pairs_v[c, zz] == own)
            total = total + jnp.dot(
                w, ibuf[c, zz].reshape(16 * ROWS, HALF), preferred_element_type=F32
            )
        return total

    images.share()
    text_sum = text_plane(core)
    for k in range(1, N_BAL):
        slots(k).wait()
    for c in range(N_BAL):
        ig_ref[c * CAP : (c + 1) * CAP, :] = ar[c]
    images.sent(0, 3)
    images.arrive(3)
    text_sum = text_sum + text_plane(1 - core)
    text_dir = scale * unpack(text_sum)
    tg_ref[...] = (
        text_dir - text_unit * jnp.sum(text_unit * text_dir, axis=1, keepdims=True)
    ) * text_scale

    images.sent(3, 4)


def deliver(ig, tg, ig_out, tg_out):
    ig_out[...] = ig[...]
    tg_out[...] = tg[...]


def body(
    patches, patch_counts, destinations, image_match, text_features,
    ln_gain, w_qkv, w_out, logit_scale, logit_bias,
):
    smem = pl.BlockSpec(memory_space=pltpu.SMEM)
    vmem = pl.BlockSpec(memory_space=pltpu.VMEM)
    hbm = pl.BlockSpec(memory_space=pl.ANY)
    dma = pltpu.SemaphoreType.DMA
    out_shape = (
        jax.ShapeDtypeStruct((N_BAL * CAP, D), F32),
        jax.ShapeDtypeStruct((SEQ, D), F32),
    )
    grads = pl.pallas_call(
        kernel,
        out_shape=out_shape,
        in_specs=[smem] * 5 + [vmem] * 2 + [hbm] * 3,
        out_specs=(vmem, vmem),
        scratch_shapes=[
            pltpu.VMEM((SEQ, L, D), BF),
            pltpu.VMEM((D, 3 * D), BF),
            pltpu.VMEM((D, D), BF),
            pltpu.VMEM((L, D), BF),
            pltpu.VMEM((L, D), BF),
            pltpu.VMEM((L, 2 * D), BF),
            pltpu.VMEM((L, 2 * D), BF),
            pltpu.VMEM((L, 128), F32),
            pltpu.VMEM((L, 128), F32),
            pltpu.VMEM((SEQ * HEADS, D), F32),
            pltpu.VMEM((SEQ, D), F32),
            pltpu.VMEM((2, 4, 4, 4, ROWS, HALF), BF),
            pltpu.VMEM((2, 4, 4, 4, ROWS, HALF), BF),
            pltpu.VMEM((ROWS, HALF), BF),
            pltpu.VMEM((ROWS, HALF), BF),
            pltpu.VMEM((2, 4, SEQ, 16 * ROWS), F32),
            pltpu.VMEM((N_BAL, CAP, D), F32),
            pltpu.VMEM((N_BAL, CAP, D), F32),
            dma((SEQ + 3,)),
            dma((48,)),
            dma((48,)),
            dma((48,)),
            dma((48,)),
            dma((N_BAL,)),
            dma((N_BAL,)),
        ],
        compiler_params=pltpu.CompilerParams(
            collective_id=0, has_side_effects=True, vmem_limit_bytes=63 * 2**20
        ),
    )(
        patch_counts, image_match, destinations.reshape(SEQ), logit_scale.reshape(1), logit_bias.reshape(1),
        ln_gain, text_features, patches, w_qkv, w_out,
    )
    return pl.pallas_call(
        deliver,
        out_shape=out_shape,
        in_specs=[vmem] * 2,
        out_specs=(vmem, vmem),
    )(*grads)


def solution(mesh):
    rows = P(("dp", "balance"))
    return jax.shard_map(
        body,
        mesh=mesh,
        in_specs=(rows,) * 5 + (P(),) * 5,
        out_specs=(rows, rows),
        check_vma=False,
    )
```
